1024 devices in a mesh: row: 16 (over x, core), col: 64 (over z, y).
Axes of the slice: x: 8, y: 8, z: 8, core: 2. Of those that a mesh axis runs over, the one named last changes fastest.
Arguments:
- fwd_now: float32 [3, 8388608], P(None, ('row', 'col')), may hold values from -6 to 6
- fwd_prev: float32 [3, 8388608], P(None, ('row', 'col')), may hold values from -6 to 6
- adj_now: float32 [3, 8388608], P(None, ('row', 'col')), may hold values from -6 to 6
- adj_prev: float32 [3, 8388608], P(None, ('row', 'col')), may hold values from -6 to 6
- inv_mass: float32 [8388608], P(('row', 'col')), may hold values from 0.1 to 1
- ibool: int32 [125, 131072], P(None, ('row', 'col')), may hold values from 0 to 8191
- inv_jac: float32 [3, 131072], P(None, ('row', 'col')), may hold values from 0.5 to 1.5
- kappa: float32 [125, 131072], P(None, ('row', 'col')), may hold values from 0.5 to 2
- mu: float32 [125, 131072], P(None, ('row', 'col')), may hold values from 0.2 to 1
- elem_count: int32 [1024], P(('row', 'col')), may hold values from 1 to 128, 98304 in all
- face_nodes: int32 [1024, 4, 640], P(('row', 'col')), may hold values from 0 to 8191
- face_len: int32 [1024, 4], P(('row', 'col')), may hold values from 0 to 640, as said below
- edge_nodes: int32 [1024, 4, 42], P(('row', 'col')), may hold values from 0 to 8191
- edge_len: int32 [1024, 4], P(('row', 'col')), may hold values from 0 to 42, as said below
- rec_elem: int32 [131072], P(('row', 'col')), may hold values from 0 to 127
- adj_src: float32 [2, 3, 131072], P(None, None, ('row', 'col')), may hold values from -24 to 24
Outputs:
- fwd_out: float32 [3, 8388608], P(None, ('row', 'col'))
- adj_out: float32 [3, 8388608], P(None, ('row', 'col'))
- rho_kernel: float32 [125, 131072], P(None, ('row', 'col'))
- kappa_kernel: float32 [125, 131072], P(None, ('row', 'col'))
- mu_kernel: float32 [125, 131072], P(None, ('row', 'col'))
The draws below stay inside these ranges and needn't reach their ends.
Inputs may be any that keep to these rules, and one draw needn't show every extreme that they name: face_len[p, s] equals the partner's length for the opposite slot, is 0 where the partner lies outside the grid and else at least 640 // 2; some pair along col has 640. edge_len[p, s] equals the partner's length for the opposite slot, is 0 where the partner lies outside the grid and else at least max(42 // 2, 1); some pair has 42.
All inputs are finite; a program needn't handle non-finite values. No bound on the sum of `elem_count` on one device may be relied on, other than what follows from the above.
Results may differ from the reference program's by a relative error of at most 0.0003.
Values sent between devices are 32-bit elements; how exact they have to be, the bound alone decides.
A program may use at most 128 MiB of HBM per device.

```python
import math
import jax
import jax.numpy as jnp
import numpy as np
from jax import lax

ELEM_DEV = 128
REC_DEV = 128
POINTS = 125
STEPS = 2
NODES_DEV = 8192
FACE_MAX = 640
EDGE_MAX = 42
PARTITIONS = 1024
ELEMENTS = 131072
NODES_ALL = 8388608
RECS = 131072
N_ROW = 16
N_COL = 64


def spread_pairs(first, second, third, fourth):
    return jnp.stack([first, second, third, fourth], 2).reshape(N_ROW * N_COL, 4)


def pair_draw(key, top, shape_rows, shape_cols, valid):
    low = max(top // 2, 1)
    key_len, key_pick = jax.random.split(key)
    values = jax.random.randint(key_len, (shape_rows, shape_cols), low, top + 1)
    flat_valid = valid.reshape(-1).astype(jnp.int32)
    order = jnp.cumsum(flat_valid) - 1
    total = jnp.sum(flat_valid)
    pick = jax.random.randint(key_pick, (), 0, 1 << 20) % total
    chosen = ((order == pick) & (flat_valid == 1)).reshape(shape_rows, shape_cols)
    values = jnp.where(chosen, top, values)
    return jnp.where(valid, values, 0)


def draw_face_len(key, part):
    key = jax.random.fold_in(key, 11)
    key_col, key_row = jax.random.split(key)
    rows = jnp.arange(N_ROW)[:, None] + jnp.zeros((1, N_COL), jnp.int32)
    cols = jnp.arange(N_COL)[None, :] + jnp.zeros((N_ROW, 1), jnp.int32)
    along_col = pair_draw(key_col, FACE_MAX, N_ROW, N_COL, cols < N_COL - 1)
    along_row = pair_draw(key_row, FACE_MAX, N_ROW, N_COL, rows < N_ROW - 1)
    return spread_pairs(along_col, jnp.roll(along_col, 1, 1), along_row, jnp.roll(along_row, 1, 0)).astype(jnp.int32)


def draw_edge_len(key, part):
    key = jax.random.fold_in(key, 23)
    key_down, key_up = jax.random.split(key)
    rows = jnp.arange(N_ROW)[:, None] + jnp.zeros((1, N_COL), jnp.int32)
    cols = jnp.arange(N_COL)[None, :] + jnp.zeros((N_ROW, 1), jnp.int32)
    diag_right = pair_draw(key_down, EDGE_MAX, N_ROW, N_COL, (rows < N_ROW - 1) & (cols < N_COL - 1))
    diag_left = pair_draw(key_up, EDGE_MAX, N_ROW, N_COL, (rows < N_ROW - 1) & (cols > 0))
    return spread_pairs(diag_right, diag_left, jnp.roll(diag_left, (1, -1), (0, 1)), jnp.roll(diag_right, (1, 1), (0, 1))).astype(jnp.int32)


def with_ends(values, own_key, low, top_value):
    extent = values.shape
    index_at = [jax.random.randint(jax.random.fold_in(own_key, axis), (), 0, extent[axis]) for axis in range(len(extent))]
    values = values.at[tuple(index_at)].set(low)
    longest = extent.index(max(extent))
    index_at[longest] = (index_at[longest] + 1) % extent[longest]
    return values.at[tuple(index_at)].set(top_value)


def block_levels(own_key, extent, shards, least, top_value):
    def one(position, blocks):
        heights = jax.random.uniform(jax.random.fold_in(jax.random.fold_in(own_key, 6), position), (blocks,), jnp.float32, least / len(shards), top_value / len(shards))
        return jnp.repeat(jnp.exp(heights), extent[position] // blocks).reshape((-1,) + (1,) * (len(extent) - position - 1))

    gain = one(*shards[0])
    for cut in shards[1:]:
        gain = gain * one(*cut)
    return gain


def split_up(number_of, total, most, lean):
    weights = [(1 << 20) // math.isqrt(standing ** lean) + 1 for standing in range(2, number_of + 1)]
    rest, holding = total - most - (number_of - 1), [1] * (number_of - 1)
    while rest > 0:
        movable = [i for i in range(number_of - 1) if holding[i] < most]
        whole, left = sum([weights[i] for i in movable]), rest
        for i in movable:
            extra = min(most - holding[i], max(1, left * weights[i] // whole), rest)
            holding[i] = holding[i] + extra
            rest = rest - extra
    return np.array([most] + holding)


def uneven(rng, number_of, total, limit, skew):
    if number_of == 2:
        one = jax.random.randint(rng, (), max(1, total - limit), min(limit, total - 1) + 1)
        return jnp.stack([one, total - one])
    sizes = jnp.asarray(split_up(number_of, total, limit, skew), jnp.int32)
    twos = (number_of - 1) // 2
    giver, receiver = sizes[1:1 + 2 * twos:2], sizes[2:2 + 2 * twos:2]
    slack = jnp.minimum(giver - 1, limit - receiver)
    passed = jax.random.randint(jax.random.fold_in(rng, 1), (twos,), 0, 1 << 20) % (slack + 1)
    sizes = sizes.at[1:1 + 2 * twos:2].set(giver - passed).at[2:2 + 2 * twos:2].set(receiver + passed)
    return sizes[jax.random.permutation(jax.random.fold_in(rng, 2), number_of)]


def scatter_about(rng, extent, spread, most, cuts=(), kind=jnp.bfloat16):
    gain = block_levels(rng, extent, cuts, -0.22, 0.18) if cuts else 1.0
    result = jax.random.normal(rng, extent, jnp.float32) * spread * gain
    return jnp.minimum(jnp.maximum(result, -most), most).astype(kind)


def setup_inputs(seed: int = 0) -> dict:
    key_list = jax.random.split(jax.random.key(seed), 17)
    fwd_now = scatter_about(key_list[0], (3, NODES_ALL), 1.0, 6.0, ((1, 1024),), jnp.float32)
    fwd_prev = scatter_about(key_list[1], (3, NODES_ALL), 1.0, 6.0, ((1, 1024),), jnp.float32)
    adj_now = scatter_about(key_list[2], (3, NODES_ALL), 1.0, 6.0, ((1, 1024),), jnp.float32)
    adj_prev = scatter_about(key_list[3], (3, NODES_ALL), 1.0, 6.0, ((1, 1024),), jnp.float32)
    inv_mass = jnp.clip(jnp.exp(math.log(1.0) - 2.3025851 * jax.random.uniform(key_list[4], (NODES_ALL,), jnp.float32) ** block_levels(key_list[4], (NODES_ALL,), ((0, 1024),), -0.2, 0.2)), 0.1, 1.0)
    ibool = with_ends(jax.random.randint(key_list[5], (POINTS, ELEMENTS), 0, NODES_DEV), jax.random.fold_in(key_list[5], 1), 0, NODES_DEV - 1).astype(jnp.int32)
    inv_jac = jnp.clip(jnp.exp(math.log(1.5) - 1.0986123 * jax.random.uniform(key_list[6], (3, ELEMENTS), jnp.float32) ** block_levels(key_list[6], (3, ELEMENTS), ((1, 1024),), -0.2, 0.2)), 0.5, 1.5)
    kappa = jnp.clip(jnp.exp(math.log(2.0) - 1.3862944 * jax.random.uniform(key_list[7], (POINTS, ELEMENTS), jnp.float32) ** block_levels(key_list[7], (POINTS, ELEMENTS), ((1, 1024),), -0.2, 0.2)), 0.5, 2.0)
    mu = jnp.clip(jnp.exp(math.log(1.0) - 1.609438 * jax.random.uniform(key_list[8], (POINTS, ELEMENTS), jnp.float32) ** block_levels(key_list[8], (POINTS, ELEMENTS), ((1, 1024),), -0.2, 0.2)), 0.2, 1.0)
    elem_count = uneven(key_list[9], PARTITIONS, PARTITIONS * ELEM_DEV * 3 // 4, ELEM_DEV, 2).astype(jnp.int32)
    face_nodes = with_ends(jax.random.randint(key_list[10], (PARTITIONS, 4, FACE_MAX), 0, NODES_DEV), jax.random.fold_in(key_list[10], 1), 0, NODES_DEV - 1).astype(jnp.int32)
    face_len = draw_face_len(jax.random.fold_in(key_list[16], 71), 0)
    edge_nodes = with_ends(jax.random.randint(key_list[12], (PARTITIONS, 4, EDGE_MAX), 0, NODES_DEV), jax.random.fold_in(key_list[12], 1), 0, NODES_DEV - 1).astype(jnp.int32)
    edge_len = draw_edge_len(jax.random.fold_in(key_list[16], 71), 0)
    rec_elem = with_ends(jax.random.randint(key_list[14], (RECS,), 0, ELEM_DEV), jax.random.fold_in(key_list[14], 1), 0, ELEM_DEV - 1).astype(jnp.int32)
    adj_src = scatter_about(key_list[15], (STEPS, 3, RECS), 4.0, 24.0, ((2, 1024),), jnp.float32)
    return dict(fwd_now=fwd_now, fwd_prev=fwd_prev, adj_now=adj_now, adj_prev=adj_prev, inv_mass=inv_mass, ibool=ibool, inv_jac=inv_jac, kappa=kappa, mu=mu, elem_count=elem_count, face_nodes=face_nodes, face_len=face_len, edge_nodes=edge_nodes, edge_len=edge_len, rec_elem=rec_elem, adj_src=adj_src)


time_step = 0.5

def gll_tables():
    points = np.array([-1.0, -math.sqrt(3.0 / 7.0), 0.0, math.sqrt(3.0 / 7.0), 1.0])
    weights = np.array([0.1, 49.0 / 90.0, 32.0 / 45.0, 49.0 / 90.0, 0.1])
    table = np.zeros((5, 5))
    for a in range(5):
        for i in range(5):
            if a != i:
                prod_a = np.prod([points[a] - points[m] for m in range(5) if m != a])
                prod_i = np.prod([points[i] - points[m] for m in range(5) if m != i])
                table[a, i] = prod_a / (prod_i * (points[a] - points[i]))
            else:
                table[a, a] = sum([1.0 / (points[a] - points[m]) for m in range(5) if m != a])
    cube = weights[:, None, None] * weights[None, :, None] * weights[None, None, :]
    return (table, cube)

def element_force(points_field, inv_jac, kappa, mu):
    table_np, cube_np = gll_tables()
    count = points_field.shape[-1]
    table = jnp.asarray(table_np, jnp.float32)
    high = lax.Precision.HIGHEST
    field = points_field.reshape(3, 5, 5, 5, count)
    scale_x, scale_y, scale_z = (inv_jac[0], inv_jac[1], inv_jac[2])
    grad_x = jnp.einsum('ai,ckjie->ckjae', table, field, precision=high) * scale_x
    grad_y = jnp.einsum('bj,ckjie->ckbie', table, field, precision=high) * scale_y
    grad_z = jnp.einsum('mk,ckjie->cmjie', table, field, precision=high) * scale_z
    grads = jnp.stack([grad_x, grad_y, grad_z], 1)
    strain = 0.5 * (grads + jnp.swapaxes(grads, 0, 1))
    div = grads[0, 0] + grads[1, 1] + grads[2, 2]
    bulk = kappa.reshape(5, 5, 5, count)
    shear = mu.reshape(5, 5, 5, count)
    ident = jnp.eye(3, dtype=jnp.float32)[:, :, None, None, None, None]
    stress = 2.0 * shear * strain + (bulk - 2.0 / 3.0 * shear) * div * ident
    weight = jnp.asarray(cube_np, jnp.float32)[..., None] / (scale_x * scale_y * scale_z)
    flux = stress * weight
    force = jnp.einsum('ai,ckjae->ckjie', table, flux[:, 0], precision=high) * scale_x
    force = force + jnp.einsum('bj,ckbie->ckjie', table, flux[:, 1], precision=high) * scale_y
    force = force + jnp.einsum('mk,cmjie->ckjie', table, flux[:, 2], precision=high) * scale_z
    deviator = strain - div / 3.0 * ident
    return (force.reshape(3, 125, count), div.reshape(125, count), deviator.reshape(3, 3, 125, count))

def from_offset(grid, drow, dcol):
    rows, cols = (grid.shape[0], grid.shape[1])
    padded = jnp.pad(grid, ((1, 1), (1, 1)) + ((0, 0),) * (grid.ndim - 2))
    return padded[1 - drow:1 - drow + rows, 1 - dcol:1 - dcol + cols]
face_offsets = ((0, 1), (0, -1), (1, 0), (-1, 0))
face_opposite = (1, 0, 3, 2)
edge_offsets = ((1, 1), (1, -1), (-1, 1), (-1, -1))
edge_opposite = (3, 2, 1, 0)

def assemble(force, lists):
    total = force
    for nodes, lengths, offsets, opposite in lists:
        width = nodes.shape[-1]
        keep = (jnp.arange(width)[None, None, :] < lengths[:, :, None]).astype(jnp.float32)
        sent = jax.vmap(lambda f, n: f[:, n])(force, nodes) * keep[:, None]
        grid = sent.reshape((N_ROW, N_COL) + sent.shape[1:])
        pieces = []
        for s in range(4):
            pieces.append(from_offset(grid[:, :, :, opposite[s]], -offsets[s][0], -offsets[s][1]))
        received = jnp.stack(pieces, 3).reshape(sent.shape)
        total = jax.vmap(lambda t, n, r: t.at[:, n].add(r))(total, nodes, received)
    return total

def reference(fwd_now, fwd_prev, adj_now, adj_prev, inv_mass, ibool, inv_jac, kappa, mu, elem_count, face_nodes, face_len, edge_nodes, edge_len, rec_elem, adj_src):
    parts = N_ROW * N_COL

    def split_nodes(a):
        return a.reshape(3, parts, NODES_DEV).transpose(1, 0, 2)

    def split_elems(a):
        return a.reshape(a.shape[0], parts, ELEM_DEV).transpose(1, 0, 2)
    forward, before_f = (split_nodes(fwd_now), split_nodes(fwd_prev))
    adjoint, before_a = (split_nodes(adj_now), split_nodes(adj_prev))
    masses = inv_mass.reshape(parts, NODES_DEV)[:, None, :]
    connect = split_elems(ibool)
    jacobian = split_elems(inv_jac)
    bulk = split_elems(kappa)
    shear = split_elems(mu)
    keeps = (jnp.arange(ELEM_DEV)[None, :] < elem_count[:, None]).astype(jnp.float32)
    recs = rec_elem.reshape(parts, REC_DEV)
    sources = adj_src.reshape(STEPS, 3, parts, REC_DEV).transpose(2, 0, 1, 3)
    lists = ((face_nodes, face_len, face_offsets, face_opposite), (edge_nodes, edge_len, edge_offsets, edge_opposite))
    rho_k = jnp.zeros((parts, 125, ELEM_DEV), jnp.float32)
    kappa_k = jnp.zeros((parts, 125, ELEM_DEV), jnp.float32)
    mu_k = jnp.zeros((parts, 125, ELEM_DEV), jnp.float32)
    for step in range(STEPS):

        def work(items):
            fwd, adj, cn, jc, kp, sh, keep, rc, src = items
            pts_f = fwd[:, cn]
            pts_a = adj[:, cn]
            force_f, div_f, dev_f = element_force(pts_f, jc, kp, sh)
            force_a, div_a, dev_a = element_force(pts_a, jc, kp, sh)
            nodes_f = jnp.zeros_like(fwd).at[:, cn].add(-force_f * keep)
            nodes_a = jnp.zeros_like(adj).at[:, cn].add(-force_a * keep)
            nodes_a = nodes_a.at[:, cn[62][rc]].add(src[step])
            kappa_inc = time_step * div_f * div_a * keep
            mu_inc = 2.0 * time_step * lax.optimization_barrier(jnp.sum(dev_f * dev_a, (0, 1))) * keep
            return (nodes_f, nodes_a, kappa_inc, mu_inc)
        local_f, local_a, kappa_inc, mu_inc = lax.map(work, (forward, adjoint, connect, jacobian, bulk, shear, keeps, recs, sources))
        total_f = assemble(local_f, lists)
        total_a = assemble(local_a, lists)
        accel_a = masses * total_a

        def density(items):
            acc, fwd, cn, keep = items
            return time_step * lax.optimization_barrier(jnp.sum(acc[:, cn] * fwd[:, cn], 0)) * keep
        rho_k = rho_k + lax.map(density, (accel_a, forward, connect, keeps))
        kappa_k = kappa_k + kappa_inc
        mu_k = mu_k + mu_inc
        next_f = 2.0 * forward - before_f + time_step * time_step * masses * total_f
        next_a = 2.0 * adjoint - before_a + time_step * time_step * masses * total_a
        before_f, forward = (forward, next_f)
        before_a, adjoint = (adjoint, next_a)

    def join_nodes(a):
        return a.transpose(1, 0, 2).reshape(3, parts * NODES_DEV)

    def join_elems(a):
        return a.transpose(1, 0, 2).reshape(125, parts * ELEM_DEV)
    return (join_nodes(forward), join_nodes(adjoint), join_elems(rho_k), join_elems(kappa_k), join_elems(mu_k))
```

```python
import functools
import math

import jax
import jax.numpy as jnp
import ml_dtypes
import numpy as np
from jax import lax
from jax.experimental import pallas as pl
from jax.experimental.pallas import tpu as pltpu
from jax.sharding import PartitionSpec as P

time_step = 0.5
F32 = jnp.float32
BF16 = jnp.bfloat16
MESH = pl.DeviceIdType.MESH

LANES = 128
HIGH_ROWS = 32
COLUMNS = 256
FIELDS = 6
TABLE = FIELDS * HIGH_ROWS
POINT_ROWS = 128
LIST_ROWS = 24
GROUP = 8
WIDE = GROUP * LANES

face_offsets = ((0, 1), (0, -1), (1, 0), (-1, 0))
face_opposite = (1, 0, 3, 2)
edge_offsets = ((1, 1), (1, -1), (-1, 1), (-1, -1))
edge_opposite = (3, 2, 1, 0)


def gll_tables():
    points = np.array([-1.0, -math.sqrt(3.0 / 7.0), 0.0, math.sqrt(3.0 / 7.0), 1.0])
    weights = np.array([0.1, 49.0 / 90.0, 32.0 / 45.0, 49.0 / 90.0, 0.1])
    table = np.zeros((5, 5))
    for a in range(5):
        for i in range(5):
            if a != i:
                prod_a = np.prod([points[a] - points[m] for m in range(5) if m != a])
                prod_i = np.prod([points[i] - points[m] for m in range(5) if m != i])
                table[a, i] = prod_a / (prod_i * (points[a] - points[i]))
            else:
                table[a, a] = sum([1.0 / (points[a] - points[m]) for m in range(5) if m != a])
    cube = weights[:, None, None] * weights[None, :, None] * weights[None, None, :]
    return (table, cube)


def operators():
    table, cube = gll_tables()
    five = np.eye(5)
    blocks = []
    for op in (
        np.kron(np.eye(25), table),
        np.kron(np.kron(five, table), five),
        np.kron(table, np.eye(25)),
    ):
        block = np.zeros((POINT_ROWS, POINT_ROWS), np.float32)
        block[:125, :125] = op
        blocks.append(block)
    forward = np.concatenate(blocks, 0)
    backward = np.concatenate([b.T for b in blocks], 1)

    def parts(a):
        high = a.astype(ml_dtypes.bfloat16)
        low = (a - high.astype(np.float32)).astype(ml_dtypes.bfloat16)
        return jnp.asarray(np.concatenate([high, high, low], 1))

    weight = np.zeros((POINT_ROWS, LANES), np.float32)
    weight[:125] = cube.reshape(125, 1)
    return (parts(forward), parts(backward), jnp.asarray(weight))


def split(value):
    high = value.astype(BF16)
    low = (value - high.astype(F32)).astype(BF16)
    return (high, low)


def build_one_hot(index_ref, rows, hot_ref, row_ref):
    def body(i, carry):
        index = index_ref[pl.ds(pl.multiple_of(i * GROUP, GROUP), GROUP), :]
        column = jnp.bitwise_and(index, 127) + jnp.left_shift(jnp.right_shift(index, 12), 7)
        high = jnp.where(index < 0, 99, jnp.bitwise_and(jnp.right_shift(index, 7), 31))
        column = column.astype(F32).astype(BF16)
        high = high.astype(F32).astype(BF16)
        columns = lax.broadcasted_iota(jnp.int32, (COLUMNS, LANES), 0).astype(F32).astype(BF16)
        highs = lax.broadcasted_iota(jnp.int32, (HIGH_ROWS, LANES), 0).astype(F32).astype(BF16)
        one, zero = (jnp.ones((), BF16), jnp.zeros((), BF16))
        for u in range(GROUP):
            at = pl.ds(pl.multiple_of(i * WIDE + u * LANES, LANES), LANES)
            here = jnp.broadcast_to(column[u : u + 1], (COLUMNS, LANES)) == columns
            hot_ref[:, at] = jnp.where(here, one, zero)
            here = jnp.broadcast_to(high[u : u + 1], (HIGH_ROWS, LANES)) == highs
            row_ref[:, at] = jnp.where(here, one, zero)
        return carry

    lax.fori_loop(0, rows // GROUP, body, 0)


def make_table(source, fields, table_ref):
    for c in range(fields):
        high, low = split(source(c))
        at = pl.ds(c * HIGH_ROWS, HIGH_ROWS)
        for b in range(2):
            part = slice(b * HIGH_ROWS, (b + 1) * HIGH_ROWS)
            table_ref[at, b * LANES : (b + 1) * LANES] = high[part]
            table_ref[at, COLUMNS + b * LANES : COLUMNS + (b + 1) * LANES] = low[part]


def gather(table_ref, fields, rows, hot_ref, row_ref, put):
    height = fields * HIGH_ROWS

    def body(i, carry):
        at = pl.ds(pl.multiple_of(i * WIDE, WIDE), WIDE)
        hot = hot_ref[:, at]
        found = jnp.dot(table_ref[:height, :COLUMNS], hot, preferred_element_type=F32)
        found += jnp.dot(table_ref[:height, COLUMNS:], hot, preferred_element_type=F32)
        mask = row_ref[:, at].astype(F32)
        for c in range(fields):
            part = found[c * HIGH_ROWS : (c + 1) * HIGH_ROWS]
            value = jnp.sum(part * mask, axis=0, keepdims=True)
            for u in range(GROUP):
                put(i, u, c, value[:, u * LANES : (u + 1) * LANES])
        return carry

    lax.fori_loop(0, rows // GROUP, body, 0)


def scatter(load, rows, hot_ref, row_ref, masked_ref, total_ref):
    def body(i, carry):
        at = pl.ds(pl.multiple_of(i * WIDE, WIDE), WIDE)
        group = load(i)
        for u in range(GROUP):
            mask = row_ref[:, pl.ds(pl.multiple_of(i * WIDE + u * LANES, LANES), LANES)]
            values = group(u)
            lanes = slice(u * LANES, (u + 1) * LANES)
            for c in range(FIELDS):
                high, low = split(values[c])
                top = c * HIGH_ROWS
                masked_ref[top : top + HIGH_ROWS, lanes] = mask * jnp.broadcast_to(
                    high, (HIGH_ROWS, LANES)
                )
                top = TABLE + c * HIGH_ROWS
                masked_ref[top : top + HIGH_ROWS, lanes] = mask * jnp.broadcast_to(
                    low, (HIGH_ROWS, LANES)
                )
        added = lax.dot_general(
            masked_ref[...],
            hot_ref[:, at],
            (((1,), (1,)), ((), ())),
            preferred_element_type=F32,
        )
        total_ref[...] += added[:TABLE] + added[TABLE:]
        return carry

    lax.fori_loop(0, rows // GROUP, body, 0)


def element_force(
    points_ref, bulk_ref, shear_ref, weight_ref, jac_ref, keep, forward_op, backward_op,
    rhs_ref, grad_ref, flux_ref, force_ref, kappa_ref, mu_ref, first,
):
    for c in range(FIELDS):
        high, low = split(points_ref[c])
        lanes = slice(c * LANES, (c + 1) * LANES)
        rhs_ref[0:128, lanes] = high
        rhs_ref[128:256, lanes] = low
        rhs_ref[256:384, lanes] = high
    grad_ref[...] = jnp.dot(forward_op[...], rhs_ref[...], preferred_element_type=F32)
    scales = [jac_ref[d : d + 1, :] for d in range(3)]
    inverse = -keep / (scales[0] * scales[1] * scales[2])

    def body(i, carry):
        tile = 16
        at = pl.ds(pl.multiple_of(i * tile, tile), tile)
        bulk, shear = (bulk_ref[at, :], shear_ref[at, :])
        weight = weight_ref[at, :] * inverse
        divs, devs = ([], [])
        for f in range(2):
            grads = [
                [
                    grad_ref[
                        pl.ds(pl.multiple_of(d * 128 + i * tile, tile), tile),
                        (f * 3 + c) * LANES : (f * 3 + c + 1) * LANES,
                    ]
                    * scales[d]
                    for d in range(3)
                ]
                for c in range(3)
            ]
            div = grads[0][0] + grads[1][1] + grads[2][2]
            lame = (bulk - 2.0 / 3.0 * shear) * div
            third = div / 3.0
            strain = {}
            for c in range(3):
                for d in range(c, 3):
                    strain[c, d] = 0.5 * (grads[c][d] + grads[d][c]) if c != d else grads[c][c]
            for c in range(3):
                for d in range(3):
                    stress = 2.0 * shear * strain[min(c, d), max(c, d)]
                    if c == d:
                        stress = stress + lame
                    high, low = split(stress * weight * scales[d])
                    lanes = slice((f * 3 + c) * LANES, (f * 3 + c + 1) * LANES)
                    for part, value in ((0, high), (1, low), (2, high)):
                        top = pl.multiple_of(part * 384 + d * 128 + i * tile, tile)
                        flux_ref[pl.ds(top, tile), lanes] = value
            divs.append(div)
            devs.append(
                {key: value - third if key[0] == key[1] else value for key, value in strain.items()}
            )
        both = 0.0
        for c in range(3):
            for d in range(c, 3):
                term = devs[0][c, d] * devs[1][c, d]
                both = both + (term if c == d else 2.0 * term)
        kappa_add = time_step * divs[0] * divs[1] * keep
        mu_add = 2.0 * time_step * both * keep
        if first:
            kappa_ref[at, :] = kappa_add
            mu_ref[at, :] = mu_add
        else:
            kappa_ref[at, :] += kappa_add
            mu_ref[at, :] += mu_add
        return carry

    lax.fori_loop(0, POINT_ROWS // 16, body, 0)
    force_ref[...] = jnp.dot(backward_op[...], flux_ref[...], preferred_element_type=F32)


def partners():
    row, col = (lax.axis_index("row"), lax.axis_index("col"))
    rows, cols = (lax.axis_size("row"), lax.axis_size("col"))

    def at(offset):
        return (
            lax.rem(row + offset[0] + rows, rows),
            lax.rem(col + offset[1] + cols, cols),
        )

    messages = []
    for s in range(4):
        messages.append((pl.ds(s * 6, 5), pl.ds(face_opposite[s] * 6, 5), at(face_offsets[s])))
    for s in range(4):
        messages.append(
            (pl.ds(s * 6 + 5, 1), pl.ds(edge_opposite[s] * 6 + 5, 1), at(edge_offsets[s]))
        )
    return messages


def kernel(
    steps, count_ref, face_len_ref, edge_len_ref,
    fwd_ref, fwd_prev_ref, adj_ref, adj_prev_ref, mass_ref, ibool_ref, jac_ref, kap_ref, mod_ref,
    face_ref, edge_ref, rec_ref, src_ref, forward_op, backward_op, weight_ref,
    fwd_out, adj_out, rho_out, kappa_out, mu_out,
    now, prev, density, index, list_index, hot, row_hot, list_hot, list_row, table, points,
    bulk, shear, rhs, grad, flux, force, masked, total, kappa_sum, mu_sum, send, recv,
    send_sem, recv_sem,
):
    messages = partners()
    barrier = pltpu.get_barrier_semaphore()
    for _, _, device in messages:
        pl.semaphore_signal(barrier, inc=1, device_id=device, device_id_type=MESH)

    lane = lax.broadcasted_iota(jnp.int32, (1, LANES), 1)
    keep = jnp.where(lane < count_ref[0], 1.0, 0.0).astype(F32)

    index[...] = jnp.full((POINT_ROWS, LANES), -1, jnp.int32)
    index[0:125, :] = ibool_ref[...]
    bulk[...] = jnp.zeros((POINT_ROWS, LANES), F32)
    bulk[0:125, :] = kap_ref[...]
    shear[...] = jnp.zeros((POINT_ROWS, LANES), F32)
    shear[0:125, :] = mod_ref[...]
    list_index[...] = jnp.full((LIST_ROWS, LANES), -1, jnp.int32)
    width = edge_ref.shape[2]
    narrow = lax.broadcasted_iota(jnp.int32, (1, width), 1)
    for s in range(4):
        for k in range(5):
            nodes = face_ref[0, s : s + 1, k * LANES : (k + 1) * LANES]
            live = lane + k * LANES < face_len_ref[0, s]
            list_index[s * 6 + k : s * 6 + k + 1, :] = jnp.where(live, nodes, -1)
        nodes = edge_ref[0, s : s + 1, :]
        live = narrow < edge_len_ref[0, s]
        list_index[s * 6 + 5 : s * 6 + 6, 0:width] = jnp.where(live, nodes, -1)

    def spread(r, carry):
        at = pl.ds(pl.multiple_of(r * LANES, LANES), LANES)
        for base, target, source in (
            (0, now, fwd_ref), (3, now, adj_ref), (0, prev, fwd_prev_ref), (3, prev, adj_prev_ref),
        ):
            value = source[:, at]
            for c in range(3):
                target[base + c, pl.ds(r, 1), :] = value[c : c + 1]
        return carry

    lax.fori_loop(0, 64, spread, 0)
    density[...] = jnp.zeros((64, LANES), F32)
    send[...] = jnp.zeros(send.shape, F32)

    build_one_hot(index, POINT_ROWS, hot, row_hot)
    build_one_hot(list_index, LIST_ROWS, list_hot, list_row)

    element = lax.broadcasted_iota(jnp.int32, (LANES, LANES), 0)
    chosen = jnp.where(
        jnp.broadcast_to(rec_ref[...], (LANES, LANES)) == element, 1.0, 0.0
    ).astype(BF16)

    for step in range(steps):
        make_table(lambda c: now[c], FIELDS, table)

        def put_point(i, u, c, value):
            at = pl.multiple_of(i * GROUP, GROUP) + u
            points[c, pl.ds(at, 1), :] = value

        gather(table, FIELDS, POINT_ROWS, hot, row_hot, put_point)
        element_force(
            points, bulk, shear, weight_ref, jac_ref, keep, forward_op, backward_op,
            rhs, grad, flux, force, kappa_sum, mu_sum, step == 0,
        )
        for c in range(3):
            high, low = split(src_ref[step, c : c + 1, :])
            rest = (src_ref[step, c : c + 1, :] - high.astype(F32) - low.astype(F32)).astype(BF16)
            stack = jnp.concatenate(
                [jnp.broadcast_to(part.astype(F32), (8, LANES)) for part in (high, low, rest)], 0
            ).astype(BF16)
            found = lax.dot_general(
                stack, chosen, (((1,), (1,)), ((), ())), preferred_element_type=F32
            )
            lanes = slice((3 + c) * LANES, (4 + c) * LANES)
            force[62:63, lanes] += found[0:1] + found[8:9] + found[16:17]

        total[...] = jnp.zeros((TABLE, COLUMNS), F32)

        def load_point(i):
            block = force[pl.ds(pl.multiple_of(i * GROUP, GROUP), GROUP), :]
            return lambda u: [block[u : u + 1, c * LANES : (c + 1) * LANES] for c in range(FIELDS)]

        scatter(load_point, POINT_ROWS, hot, row_hot, masked, total)

        high, low = split(total[...])
        table[:, :COLUMNS] = high
        table[:, COLUMNS:] = low

        def put_list(i, u, c, value):
            send[step, i * GROUP + u, c : c + 1, :] = value

        gather(table, FIELDS, LIST_ROWS, list_hot, list_row, put_list)

        if step == 0:
            pl.semaphore_wait(barrier, len(messages))
        copies = []
        for slot, (source, target, device) in enumerate(messages):
            landing = face_opposite[slot] if slot < 4 else 4 + edge_opposite[slot - 4]
            copy = pltpu.make_async_remote_copy(
                src_ref=send.at[step, source],
                dst_ref=recv.at[step, target],
                send_sem=send_sem.at[step, slot],
                recv_sem=recv_sem.at[step, landing],
                device_id=device,
                device_id_type=MESH,
            )
            copy.start()
            copies.append(copy)
        for copy in copies:
            copy.wait()

        def load_list(i):
            return lambda u: [recv[step, i * GROUP + u, c : c + 1, :] for c in range(FIELDS)]

        scatter(load_list, LIST_ROWS, list_hot, list_row, masked, total)

        for b in range(2):
            part = pl.ds(b * HIGH_ROWS, HIGH_ROWS)
            lanes = slice(b * LANES, (b + 1) * LANES)
            mass = mass_ref[part, :]
            accel = [
                mass * total[c * HIGH_ROWS : (c + 1) * HIGH_ROWS, lanes] for c in range(FIELDS)
            ]
            both = 0.0
            for c in range(3):
                both = both + accel[3 + c] * now[c, part, :]
            density[part, :] += time_step * both
            for c in range(FIELDS):
                field = now[c, part, :]
                later = 2.0 * field - prev[c, part, :] + time_step * time_step * accel[c]
                prev[c, part, :] = field
                now[c, part, :] = later

    def join(r, carry):
        at = pl.ds(pl.multiple_of(r * LANES, LANES), LANES)
        for base, target in ((0, fwd_out), (3, adj_out)):
            for c in range(3):
                target[c : c + 1, at] = now[base + c, pl.ds(r, 1), :]
        return carry

    lax.fori_loop(0, 64, join, 0)
    make_table(lambda c: density[...], 1, table)

    def put_density(i, u, c, value):
        at = pl.multiple_of(i * GROUP, GROUP) + u
        points[0, pl.ds(at, 1), :] = value

    gather(table, 1, POINT_ROWS, hot, row_hot, put_density)
    rho_out[...] = points[0, 0:125, :] * keep
    kappa_out[...] = kappa_sum[0:125, :]
    mu_out[...] = mu_sum[0:125, :]


def on_device(
    fwd_now, fwd_prev, adj_now, adj_prev, inv_mass, ibool, inv_jac, kappa, mu, elem_count,
    face_nodes, face_len, edge_nodes, edge_len, rec_elem, adj_src,
):
    forward_op, backward_op, weight = operators()
    steps = adj_src.shape[0]
    nodes = fwd_now.shape[1]
    elements = ibool.shape[1]
    vmem = pl.BlockSpec(memory_space=pltpu.VMEM)
    smem = pl.BlockSpec(memory_space=pltpu.SMEM)
    spread = POINT_ROWS * LANES
    listed = LIST_ROWS * LANES
    scratch = [
        pltpu.VMEM((FIELDS, 64, LANES), F32),
        pltpu.VMEM((FIELDS, 64, LANES), F32),
        pltpu.VMEM((64, LANES), F32),
        pltpu.VMEM((POINT_ROWS, LANES), jnp.int32),
        pltpu.VMEM((LIST_ROWS, LANES), jnp.int32),
        pltpu.VMEM((COLUMNS, spread), BF16),
        pltpu.VMEM((HIGH_ROWS, spread), BF16),
        pltpu.VMEM((COLUMNS, listed), BF16),
        pltpu.VMEM((HIGH_ROWS, listed), BF16),
        pltpu.VMEM((TABLE, 2 * COLUMNS), BF16),
        pltpu.VMEM((FIELDS, POINT_ROWS, LANES), F32),
        pltpu.VMEM((POINT_ROWS, LANES), F32),
        pltpu.VMEM((POINT_ROWS, LANES), F32),
        pltpu.VMEM((384, FIELDS * LANES), BF16),
        pltpu.VMEM((384, FIELDS * LANES), F32),
        pltpu.VMEM((3 * 384, FIELDS * LANES), BF16),
        pltpu.VMEM((POINT_ROWS, FIELDS * LANES), F32),
        pltpu.VMEM((2 * TABLE, WIDE), BF16),
        pltpu.VMEM((TABLE, COLUMNS), F32),
        pltpu.VMEM((POINT_ROWS, LANES), F32),
        pltpu.VMEM((POINT_ROWS, LANES), F32),
        pltpu.VMEM((steps, LIST_ROWS, 8, LANES), F32),
        pltpu.VMEM((steps, LIST_ROWS, 8, LANES), F32),
        pltpu.SemaphoreType.DMA((steps, 8)),
        pltpu.SemaphoreType.DMA((steps, 8)),
    ]
    point = jax.ShapeDtypeStruct((125, elements), F32)
    node = jax.ShapeDtypeStruct((3, nodes), F32)
    return pl.pallas_call(
        functools.partial(kernel, steps),
        out_shape=(node, node, point, point, point),
        in_specs=[smem] * 3 + [vmem] * 16,
        out_specs=(vmem,) * 5,
        scratch_shapes=scratch,
        compiler_params=pltpu.CompilerParams(
            collective_id=0, has_side_effects=True, vmem_limit_bytes=40 << 20
        ),
    )(
        elem_count, face_len, edge_len,
        fwd_now, fwd_prev, adj_now, adj_prev, inv_mass.reshape(64, LANES), ibool, inv_jac, kappa, mu,
        face_nodes, edge_nodes, rec_elem.reshape(1, elements), adj_src,
        forward_op, backward_op, weight,
    )


def solution(mesh):
    field = P(None, ("row", "col"))
    part = P(("row", "col"))
    in_specs = (
        field, field, field, field, part, field, field, field, field, part,
        P(("row", "col"), None, None), P(("row", "col"), None),
        P(("row", "col"), None, None), P(("row", "col"), None),
        part, P(None, None, ("row", "col")),
    )
    return jax.shard_map(
        on_device, mesh=mesh, in_specs=in_specs, out_specs=(field,) * 5, check_vma=False
    )
```

```python
import functools
import math

import jax
import jax.numpy as jnp
import ml_dtypes
import numpy as np
from jax import lax
from jax.experimental import pallas as pl
from jax.experimental.pallas import tpu as pltpu
from jax.sharding import PartitionSpec as P

time_step = 0.5
F32 = jnp.float32
BF16 = jnp.bfloat16
MESH = pl.DeviceIdType.MESH

LANES = 128
HIGH_ROWS = 32
COLUMNS = 256
FIELDS = 6
TABLE = FIELDS * HIGH_ROWS
POINT_ROWS = 128
LIST_ROWS = 24
GROUP = 8
WIDE = GROUP * LANES
GATHER_ROWS = 64
SCATTER_ROWS = 64

face_offsets = ((0, 1), (0, -1), (1, 0), (-1, 0))
face_opposite = (1, 0, 3, 2)
edge_offsets = ((1, 1), (1, -1), (-1, 1), (-1, -1))
edge_opposite = (3, 2, 1, 0)


def gll_tables():
    points = np.array([-1.0, -math.sqrt(3.0 / 7.0), 0.0, math.sqrt(3.0 / 7.0), 1.0])
    weights = np.array([0.1, 49.0 / 90.0, 32.0 / 45.0, 49.0 / 90.0, 0.1])
    table = np.zeros((5, 5))
    for a in range(5):
        for i in range(5):
            if a != i:
                prod_a = np.prod([points[a] - points[m] for m in range(5) if m != a])
                prod_i = np.prod([points[i] - points[m] for m in range(5) if m != i])
                table[a, i] = prod_a / (prod_i * (points[a] - points[i]))
            else:
                table[a, a] = sum([1.0 / (points[a] - points[m]) for m in range(5) if m != a])
    cube = weights[:, None, None] * weights[None, :, None] * weights[None, None, :]
    return (table, cube)


def operators():
    table, cube = gll_tables()
    five = np.eye(5)
    blocks = []
    for op in (
        np.kron(np.eye(25), table),
        np.kron(np.kron(five, table), five),
        np.kron(table, np.eye(25)),
    ):
        block = np.zeros((POINT_ROWS, POINT_ROWS), np.float32)
        block[:125, :125] = op
        blocks.append(block)
    forward = np.concatenate(blocks, 0)
    backward = np.concatenate([b.T for b in blocks], 1)

    def parts(a):
        high = a.astype(ml_dtypes.bfloat16)
        low = (a - high.astype(np.float32)).astype(ml_dtypes.bfloat16)
        return jnp.asarray(np.concatenate([high, high, low], 1))

    weight = np.zeros((POINT_ROWS, LANES), np.float32)
    weight[:125] = cube.reshape(125, 1)
    return (parts(forward), parts(backward), jnp.asarray(weight))


def split(value):
    high = value.astype(BF16)
    low = (value - high.astype(F32)).astype(BF16)
    return (high, low)


def build_one_hot(index_ref, rows, hot_ref, row_ref):
    def body(i, carry):
        index = index_ref[pl.ds(pl.multiple_of(i * GROUP, GROUP), GROUP), :]
        column = jnp.bitwise_and(index, 127) + jnp.left_shift(jnp.right_shift(index, 12), 7)
        high = jnp.where(index < 0, 99, jnp.bitwise_and(jnp.right_shift(index, 7), 31))
        column = column.astype(F32).astype(BF16)
        high = high.astype(F32).astype(BF16)
        columns = lax.broadcasted_iota(jnp.int32, (COLUMNS, LANES), 0).astype(F32).astype(BF16)
        highs = lax.broadcasted_iota(jnp.int32, (HIGH_ROWS, LANES), 0).astype(F32).astype(BF16)
        one, zero = (jnp.ones((), BF16), jnp.zeros((), BF16))
        for u in range(GROUP):
            at = pl.ds(pl.multiple_of(i * WIDE + u * LANES, LANES), LANES)
            here = jnp.broadcast_to(column[u : u + 1], (COLUMNS, LANES)) == columns
            hot_ref[:, at] = jnp.where(here, one, zero)
            here = jnp.broadcast_to(high[u : u + 1], (HIGH_ROWS, LANES)) == highs
            row_ref[:, at] = jnp.where(here, one, zero)
        return carry

    lax.fori_loop(0, rows // GROUP, body, 0)


def make_table(source, fields, table_ref):
    for c in range(fields):
        for k, value in enumerate(split(source(c))):
            at = pl.ds((k * fields + c) * HIGH_ROWS, HIGH_ROWS)
            for b in range(2):
                part = slice(b * HIGH_ROWS, (b + 1) * HIGH_ROWS)
                table_ref[at, b * LANES : (b + 1) * LANES] = value[part]


def sum_rows(parts):
    row = lax.broadcasted_iota(jnp.int32, (GROUP, LANES), 0)

    def merge(first, second, bit):
        own = jnp.bitwise_and(row, bit) == 0
        return jnp.where(own, first, second) + pltpu.roll(jnp.where(own, second, first), bit, 0)

    parts = [merge(parts[u], parts[u + 1], 1) for u in range(0, 8, 2)]
    parts = [merge(parts[0], parts[1], 2), merge(parts[2], parts[3], 2)]
    return merge(parts[0], parts[1], 4)


def gather(table_ref, fields, rows, chunk, hot_ref, row_ref, put):
    height = fields * HIGH_ROWS

    def body(j, carry):
        start = pl.multiple_of(j * chunk * LANES, LANES)
        found = jnp.dot(
            table_ref[: 2 * height, :],
            hot_ref[:, pl.ds(start, chunk * LANES)],
            preferred_element_type=F32,
        )
        for g in range(chunk // GROUP):
            sums = [[] for c in range(fields)]
            for u in range(GROUP):
                at = (g * GROUP + u) * LANES
                lanes = slice(at, at + LANES)
                mask = row_ref[:, pl.ds(pl.multiple_of(start + at, LANES), LANES)].astype(F32)
                for c in range(fields):
                    top = c * HIGH_ROWS
                    part = found[top : top + HIGH_ROWS, lanes]
                    part = part + found[height + top : height + top + HIGH_ROWS, lanes]
                    part = part * mask
                    sums[c].append((part[0:8] + part[8:16]) + (part[16:24] + part[24:32]))
            for c in range(fields):
                put(j * (chunk // GROUP) + g, c, sum_rows(sums[c]))
        return carry

    if rows == chunk:
        body(0, 0)
    else:
        lax.fori_loop(0, rows // chunk, body, 0)


def scatter(load, rows, chunk, hot_ref, row_ref, masked_ref, total_ref):
    def body(j, carry):
        start = pl.multiple_of(j * chunk * LANES, LANES)

        def fill(i, carry):
            group = load(j * (chunk // GROUP) + i)
            for u in range(GROUP):
                at = pl.multiple_of(i * WIDE + u * LANES, LANES)
                mask = row_ref[:, pl.ds(pl.multiple_of(start + at, LANES), LANES)]
                for c in range(FIELDS):
                    for k, value in enumerate(group(u, c)):
                        top = k * TABLE + c * HIGH_ROWS
                        masked_ref[top : top + HIGH_ROWS, pl.ds(at, LANES)] = (
                            mask * jnp.broadcast_to(value, (HIGH_ROWS, LANES))
                        )
            return carry

        lax.fori_loop(0, chunk // GROUP, fill, 0, unroll=True)
        found = lax.dot_general(
            masked_ref[:, : chunk * LANES],
            hot_ref[:, pl.ds(start, chunk * LANES)],
            (((1,), (1,)), ((), ())),
            preferred_element_type=F32,
        )
        total_ref[...] += found[:TABLE] + found[TABLE:]
        return carry

    if rows == chunk:
        body(0, 0)
    else:
        lax.fori_loop(0, rows // chunk, body, 0)


def strains(grad_ref, scales, i, tile, f):
    grads = [
        [
            grad_ref[
                pl.ds(pl.multiple_of(d * POINT_ROWS + i * tile, tile), tile),
                (f * 3 + c) * LANES : (f * 3 + c + 1) * LANES,
            ]
            * scales[d]
            for d in range(3)
        ]
        for c in range(3)
    ]
    strain = {}
    for c in range(3):
        for d in range(c, 3):
            strain[c, d] = 0.5 * (grads[c][d] + grads[d][c]) if c != d else grads[c][c]
    return (strain[0, 0] + strain[1, 1] + strain[2, 2], strain)


def element_force(
    points_ref, bulk_ref, shear_ref, weight_ref, scales, keep, forward_op, backward_op,
    rhs_ref, grad_ref, flux_ref, force_ref,
):
    for c in range(FIELDS):
        high, low = split(points_ref[c])
        lanes = slice(c * LANES, (c + 1) * LANES)
        rhs_ref[0:128, lanes] = high
        rhs_ref[128:256, lanes] = low
        rhs_ref[256:384, lanes] = high
    grad_ref[...] = jnp.dot(forward_op[...], rhs_ref[...], preferred_element_type=F32)
    inverse = -keep / (scales[0] * scales[1] * scales[2])

    def body(i, carry):
        tile = 16
        at = pl.ds(pl.multiple_of(i * tile, tile), tile)
        weight = weight_ref[at, :] * inverse
        double = 2.0 * shear_ref[at, :] * weight
        lame = (bulk_ref[at, :] - 2.0 / 3.0 * shear_ref[at, :]) * weight
        for f in range(2):
            div, strain = strains(grad_ref, scales, i, tile, f)
            for c in range(3):
                for d in range(c, 3):
                    stress = double * strain[c, d]
                    if c == d:
                        stress = stress + lame * div
                    for e, g in ((c, d), (d, c))[: 1 + (c != d)]:
                        high, low = split(stress * scales[g])
                        lanes = slice((f * 3 + e) * LANES, (f * 3 + e + 1) * LANES)
                        for part, value in ((0, high), (1, low), (2, high)):
                            top = pl.multiple_of(part * 384 + g * POINT_ROWS + i * tile, tile)
                            flux_ref[pl.ds(top, tile), lanes] = value
        return carry

    lax.fori_loop(0, POINT_ROWS // 16, body, 0, unroll=4)
    force_ref[...] = jnp.dot(backward_op[...], flux_ref[...], preferred_element_type=F32)


def add_moduli_kernels(grad_ref, scales, keep, kappa_ref, mu_ref):
    def body(i, carry):
        tile = 16
        at = pl.ds(pl.multiple_of(i * tile, tile), tile)
        divs, devs = ([], [])
        for f in range(2):
            div, strain = strains(grad_ref, scales, i, tile, f)
            third = div / 3.0
            divs.append(div)
            devs.append({k: v - third if k[0] == k[1] else v for k, v in strain.items()})
        even = sum(devs[0][c, c] * devs[1][c, c] for c in range(3))
        odd = sum(devs[0][key] * devs[1][key] for key in ((0, 1), (0, 2), (1, 2)))
        kappa_ref[at, :] += time_step * divs[0] * divs[1] * keep
        mu_ref[at, :] += 2.0 * time_step * (even + 2.0 * odd) * keep
        return carry

    lax.fori_loop(0, POINT_ROWS // 16, body, 0, unroll=4)


def partners():
    row, col = (lax.axis_index("row"), lax.axis_index("col"))
    rows, cols = (lax.axis_size("row"), lax.axis_size("col"))

    def at(offset):
        return (
            lax.rem(row + offset[0] + rows, rows),
            lax.rem(col + offset[1] + cols, cols),
        )

    messages = []
    for s in range(4):
        messages.append((pl.ds(s * 6, 5), pl.ds(face_opposite[s] * 6, 5), at(face_offsets[s])))
    for s in range(4):
        messages.append(
            (pl.ds(s * 6 + 5, 1), pl.ds(edge_opposite[s] * 6 + 5, 1), at(edge_offsets[s]))
        )
    return messages


def kernel(
    steps, count_ref, face_len_ref, edge_len_ref,
    fwd_hbm, fwd_prev_hbm, adj_hbm, adj_prev_hbm, mass_hbm, ibool_hbm, jac_hbm, kap_hbm, mod_hbm,
    face_hbm, edge_hbm, rec_hbm, src_hbm, forward_hbm, backward_hbm, weight_hbm,
    packed,
    fwd_ref, fwd_prev_ref, adj_ref, adj_prev_ref, mass_ref, ibool_ref, jac_ref, kap_ref, mod_ref,
    face_ref, edge_ref, rec_ref, src_ref, forward_op, backward_op, weight_ref,
    now, prev, density, index, list_index, hot, row_hot, list_hot, list_row, table, points,
    bulk, shear, rhs, grad, flux, force, masked, total, kappa_sum, mu_sum, send, recv,
    in_sem, send_sem, recv_sem,
):
    arrivals = []
    for source, target in (
        (ibool_hbm, ibool_ref), (face_hbm, face_ref), (edge_hbm, edge_ref), (fwd_hbm, fwd_ref),
        (adj_hbm, adj_ref), (fwd_prev_hbm, fwd_prev_ref), (adj_prev_hbm, adj_prev_ref),
        (kap_hbm, kap_ref), (mod_hbm, mod_ref), (jac_hbm, jac_ref), (weight_hbm, weight_ref),
        (forward_hbm, forward_op), (backward_hbm, backward_op), (rec_hbm, rec_ref),
        (src_hbm, src_ref), (mass_hbm, mass_ref),
    ):
        copy = pltpu.make_async_copy(source, target, in_sem.at[len(arrivals)])
        copy.start()
        arrivals.append(copy)

    messages = partners()
    barrier = pltpu.get_barrier_semaphore()
    for _, _, device in messages:
        pl.semaphore_signal(barrier, inc=1, device_id=device, device_id_type=MESH)

    lane = lax.broadcasted_iota(jnp.int32, (1, LANES), 1)
    keep = jnp.where(lane < count_ref[0], 1.0, 0.0).astype(F32)
    index[...] = jnp.full((POINT_ROWS, LANES), -1, jnp.int32)
    list_index[...] = jnp.full((LIST_ROWS, LANES), -1, jnp.int32)
    bulk[...] = jnp.zeros((POINT_ROWS, LANES), F32)
    shear[...] = jnp.zeros((POINT_ROWS, LANES), F32)
    density[...] = jnp.zeros((64, LANES), F32)
    kappa_sum[...] = jnp.zeros((POINT_ROWS, LANES), F32)
    mu_sum[...] = jnp.zeros((POINT_ROWS, LANES), F32)
    send[...] = jnp.zeros(send.shape, F32)

    arrivals[0].wait()
    index[0:125, :] = ibool_ref[...]
    build_one_hot(index, POINT_ROWS, hot, row_hot)
    for copy in arrivals[1:]:
        copy.wait()

    width = edge_ref.shape[2]
    narrow = lax.broadcasted_iota(jnp.int32, (1, width), 1)
    for s in range(4):
        for k in range(5):
            nodes = face_ref[0, s : s + 1, k * LANES : (k + 1) * LANES]
            live = lane + k * LANES < face_len_ref[0, s]
            list_index[s * 6 + k : s * 6 + k + 1, :] = jnp.where(live, nodes, -1)
        nodes = edge_ref[0, s : s + 1, :]
        live = narrow < edge_len_ref[0, s]
        list_index[s * 6 + 5 : s * 6 + 6, 0:width] = jnp.where(live, nodes, -1)
    build_one_hot(list_index, LIST_ROWS, list_hot, list_row)
    bulk[0:125, :] = kap_ref[...]
    shear[0:125, :] = mod_ref[...]

    def spread(r, carry):
        at = pl.ds(pl.multiple_of(r * LANES, LANES), LANES)
        for base, target, source in (
            (0, now, fwd_ref), (3, now, adj_ref), (0, prev, fwd_prev_ref), (3, prev, adj_prev_ref),
        ):
            value = source[:, at]
            for c in range(3):
                target[base + c, pl.ds(r, 1), :] = value[c : c + 1]
        return carry

    lax.fori_loop(0, 64, spread, 0, unroll=8)

    element = lax.broadcasted_iota(jnp.int32, (LANES, LANES), 0)
    chosen = jnp.where(
        jnp.broadcast_to(rec_ref[...], (LANES, LANES)) == element, 1.0, 0.0
    ).astype(BF16)

    def put_point(i, c, value):
        points[c, pl.ds(pl.multiple_of(i * GROUP, GROUP), GROUP), :] = value

    scales = [jac_ref[d : d + 1, :] for d in range(3)]
    pl.semaphore_wait(barrier, len(messages))

    def one_step(step, carry):
        make_table(lambda c: now[c], FIELDS, table)
        gather(table, FIELDS, POINT_ROWS, GATHER_ROWS, hot, row_hot, put_point)
        element_force(
            points, bulk, shear, weight_ref, scales, keep, forward_op, backward_op,
            rhs, grad, flux, force,
        )
        for c in range(3):
            source = src_ref[c, pl.ds(step, 1), :]
            high, low = split(source)
            rest = source - high.astype(F32) - low.astype(F32)
            stack = jnp.concatenate(
                [
                    jnp.broadcast_to(part.astype(F32), (8, LANES))
                    for part in (high, low, rest)
                ],
                0,
            ).astype(BF16)
            found = lax.dot_general(
                stack, chosen, (((1,), (1,)), ((), ())), preferred_element_type=F32
            )
            lanes = slice((3 + c) * LANES, (4 + c) * LANES)
            force[62:63, lanes] += found[0:1] + found[8:9] + found[16:17]

        def load_point(i):
            at = pl.ds(pl.multiple_of(i * GROUP, GROUP), GROUP)
            blocks = [split(force[at, c * LANES : (c + 1) * LANES]) for c in range(FIELDS)]
            return lambda u, c: [part[u : u + 1] for part in blocks[c]]

        total[...] = jnp.zeros((TABLE, COLUMNS), F32)
        scatter(load_point, POINT_ROWS, SCATTER_ROWS, hot, row_hot, masked, total)
        high, low = split(total[...])
        table[:TABLE, :] = high
        table[TABLE:, :] = low

        def put_list(i, c, value):
            for u in range(GROUP):
                send[step, i * GROUP + u, c : c + 1, :] = value[u : u + 1]

        gather(table, FIELDS, LIST_ROWS, LIST_ROWS, list_hot, list_row, put_list)

        copies = []
        for slot, (source, target, device) in enumerate(messages):
            landing = face_opposite[slot] if slot < 4 else 4 + edge_opposite[slot - 4]
            copy = pltpu.make_async_remote_copy(
                src_ref=send.at[step, source],
                dst_ref=recv.at[step, target],
                send_sem=send_sem.at[step, slot],
                recv_sem=recv_sem.at[step, landing],
                device_id=device,
                device_id_type=MESH,
            )
            copy.start()
            copies.append(copy)
        add_moduli_kernels(grad, scales, keep, kappa_sum, mu_sum)
        for copy in copies:
            copy.wait_recv()

        def load_list(i):
            blocks = [split(recv[step, i * GROUP + u]) for u in range(GROUP)]
            return lambda u, c: [part[c : c + 1] for part in blocks[u]]

        scatter(load_list, LIST_ROWS, LIST_ROWS, list_hot, list_row, masked, total)

        for b in range(2):
            part = pl.ds(b * HIGH_ROWS, HIGH_ROWS)
            lanes = slice(b * LANES, (b + 1) * LANES)
            mass = mass_ref[part, :]
            accel = [
                mass * total[c * HIGH_ROWS : (c + 1) * HIGH_ROWS, lanes] for c in range(FIELDS)
            ]
            both = 0.0
            for c in range(3):
                both = both + accel[3 + c] * now[c, part, :]
            density[part, :] += time_step * both
            for c in range(FIELDS):
                field = now[c, part, :]
                later = 2.0 * field - prev[c, part, :] + time_step * time_step * accel[c]
                prev[c, part, :] = field
                now[c, part, :] = later
        for copy in copies:
            copy.wait_send()
        return carry

    lax.fori_loop(0, steps, one_step, 0)

    make_table(lambda c: density[...], 1, table)
    gather(table, 1, POINT_ROWS, GATHER_ROWS, hot, row_hot, put_point)
    for c in range(FIELDS):
        packed[c * 64 : (c + 1) * 64, :] = now[c]
    for k, value in enumerate((points[0] * keep, kappa_sum[...], mu_sum[...])):
        packed[FIELDS * 64 + k * POINT_ROWS : FIELDS * 64 + (k + 1) * POINT_ROWS, :] = value


def unpack(
    packed, fwd_out, adj_out, rho_out, kappa_out, mu_out, fwd, adj, rho, kappa, mu, out_sem
):
    copies = []
    for k, (source, target) in enumerate(((rho, rho_out), (kappa, kappa_out), (mu, mu_out))):
        top = FIELDS * 64 + k * POINT_ROWS
        source[...] = packed[top : top + 125, :]
        copies.append(pltpu.make_async_copy(source, target, out_sem.at[k]))
        copies[k].start()
    for k, (source, target) in enumerate(((fwd, fwd_out), (adj, adj_out))):
        for c in range(3):

            def join(i, carry):
                top = (k * 3 + c) * 64 + i * GROUP
                rows = packed[pl.ds(pl.multiple_of(top, GROUP), GROUP), :]
                for u in range(GROUP):
                    at = pl.ds(pl.multiple_of(i * WIDE + u * LANES, LANES), LANES)
                    source[c : c + 1, at] = rows[u : u + 1]
                return carry

            lax.fori_loop(0, 64 // GROUP, join, 0)
        copies.append(pltpu.make_async_copy(source, target, out_sem.at[3 + k]))
        copies[3 + k].start()
    for copy in copies:
        copy.wait()


def on_device(
    fwd_now, fwd_prev, adj_now, adj_prev, inv_mass, ibool, inv_jac, kappa, mu, elem_count,
    face_nodes, face_len, edge_nodes, edge_len, rec_elem, adj_src,
):
    forward_op, backward_op, weight = operators()
    steps = adj_src.shape[0]
    nodes = fwd_now.shape[1]
    elements = ibool.shape[1]
    vmem = pl.BlockSpec(memory_space=pltpu.VMEM)
    smem = pl.BlockSpec(memory_space=pltpu.SMEM)
    spread = POINT_ROWS * LANES
    listed = LIST_ROWS * LANES
    operands = (
        fwd_now, fwd_prev, adj_now, adj_prev, inv_mass.reshape(64, LANES), ibool, inv_jac, kappa, mu,
        face_nodes, edge_nodes, rec_elem.reshape(1, elements), adj_src.transpose(1, 0, 2),
        forward_op, backward_op, weight,
    )
    scratch = [pltpu.VMEM(operand.shape, operand.dtype) for operand in operands] + [
        pltpu.VMEM((FIELDS, 64, LANES), F32),
        pltpu.VMEM((FIELDS, 64, LANES), F32),
        pltpu.VMEM((64, LANES), F32),
        pltpu.VMEM((POINT_ROWS, LANES), jnp.int32),
        pltpu.VMEM((LIST_ROWS, LANES), jnp.int32),
        pltpu.VMEM((COLUMNS, spread), BF16),
        pltpu.VMEM((HIGH_ROWS, spread), BF16),
        pltpu.VMEM((COLUMNS, listed), BF16),
        pltpu.VMEM((HIGH_ROWS, listed), BF16),
        pltpu.VMEM((2 * TABLE, COLUMNS), BF16),
        pltpu.VMEM((FIELDS, POINT_ROWS, LANES), F32),
        pltpu.VMEM((POINT_ROWS, LANES), F32),
        pltpu.VMEM((POINT_ROWS, LANES), F32),
        pltpu.VMEM((384, FIELDS * LANES), BF16),
        pltpu.VMEM((384, FIELDS * LANES), F32),
        pltpu.VMEM((3 * 384, FIELDS * LANES), BF16),
        pltpu.VMEM((POINT_ROWS, FIELDS * LANES), F32),
        pltpu.VMEM((2 * TABLE, SCATTER_ROWS * LANES), BF16),
        pltpu.VMEM((TABLE, COLUMNS), F32),
        pltpu.VMEM((POINT_ROWS, LANES), F32),
        pltpu.VMEM((POINT_ROWS, LANES), F32),
        pltpu.VMEM((steps, LIST_ROWS, 8, LANES), F32),
        pltpu.VMEM((steps, LIST_ROWS, 8, LANES), F32),
        pltpu.SemaphoreType.DMA((len(operands),)),
        pltpu.SemaphoreType.DMA((steps, 8)),
        pltpu.SemaphoreType.DMA((steps, 8)),
    ]
    point = jax.ShapeDtypeStruct((125, elements), F32)
    node = jax.ShapeDtypeStruct((3, nodes), F32)
    hbm = pl.BlockSpec(memory_space=pl.ANY)
    packed = pl.pallas_call(
        functools.partial(kernel, steps),
        out_shape=jax.ShapeDtypeStruct((FIELDS * 64 + 3 * POINT_ROWS, LANES), F32),
        in_specs=[smem] * 3 + [hbm] * len(operands),
        out_specs=vmem,
        scratch_shapes=scratch,
        compiler_params=pltpu.CompilerParams(
            collective_id=0, has_side_effects=True, vmem_limit_bytes=60 << 20
        ),
    )(elem_count, face_len, edge_len, *operands)
    outs = (node, node, point, point, point)
    return pl.pallas_call(
        unpack,
        out_shape=outs,
        in_specs=[vmem],
        out_specs=(hbm,) * 5,
        scratch_shapes=[pltpu.VMEM(out.shape, F32) for out in outs]
        + [pltpu.SemaphoreType.DMA((len(outs),))],
        compiler_params=pltpu.CompilerParams(vmem_limit_bytes=60 << 20),
    )(packed)


def solution(mesh):
    field = P(None, ("row", "col"))
    part = P(("row", "col"))
    in_specs = (
        field, field, field, field, part, field, field, field, field, part,
        P(("row", "col"), None, None), P(("row", "col"), None),
        P(("row", "col"), None, None), P(("row", "col"), None),
        part, P(None, None, ("row", "col")),
    )
    return jax.shard_map(
        on_device, mesh=mesh, in_specs=in_specs, out_specs=(field,) * 5, check_vma=False
    )
```

```python
import functools
import math

import jax
import jax.numpy as jnp
import ml_dtypes
import numpy as np
from jax import lax
from jax.experimental import pallas as pl
from jax.experimental.pallas import tpu as pltpu
from jax.sharding import PartitionSpec as P

time_step = 0.5
F32 = jnp.float32
BF16 = jnp.bfloat16
MESH = pl.DeviceIdType.MESH

LANES = 128
HIGH_ROWS = 32
COLUMNS = 256
FIELDS = 6
TABLE = FIELDS * HIGH_ROWS
POINT_ROWS = 128
LIST_ROWS = 24
GROUP = 8
WIDE = GROUP * LANES
GATHER_ROWS = 128
SCATTER_ROWS = 64

face_offsets = ((0, 1), (0, -1), (1, 0), (-1, 0))
face_opposite = (1, 0, 3, 2)
edge_offsets = ((1, 1), (1, -1), (-1, 1), (-1, -1))
edge_opposite = (3, 2, 1, 0)


def gll_tables():
    points = np.array([-1.0, -math.sqrt(3.0 / 7.0), 0.0, math.sqrt(3.0 / 7.0), 1.0])
    weights = np.array([0.1, 49.0 / 90.0, 32.0 / 45.0, 49.0 / 90.0, 0.1])
    table = np.zeros((5, 5))
    for a in range(5):
        for i in range(5):
            if a != i:
                prod_a = np.prod([points[a] - points[m] for m in range(5) if m != a])
                prod_i = np.prod([points[i] - points[m] for m in range(5) if m != i])
                table[a, i] = prod_a / (prod_i * (points[a] - points[i]))
            else:
                table[a, a] = sum([1.0 / (points[a] - points[m]) for m in range(5) if m != a])
    cube = weights[:, None, None] * weights[None, :, None] * weights[None, None, :]
    return (table, cube)


def operators():
    table, cube = gll_tables()
    five = np.eye(5)
    blocks = []
    for op in (
        np.kron(np.eye(25), table),
        np.kron(np.kron(five, table), five),
        np.kron(table, np.eye(25)),
    ):
        block = np.zeros((POINT_ROWS, POINT_ROWS), np.float32)
        block[:125, :125] = op
        blocks.append(block)
    forward = np.concatenate(blocks, 0)
    backward = np.concatenate([b.T for b in blocks], 1)

    def parts(a):
        high = a.astype(ml_dtypes.bfloat16)
        low = (a - high.astype(np.float32)).astype(ml_dtypes.bfloat16)
        return jnp.asarray(np.concatenate([high, high, low], 1))

    weight = np.zeros((POINT_ROWS, LANES), np.float32)
    weight[:125] = cube.reshape(125, 1)
    return (parts(forward), parts(backward), jnp.asarray(weight))


def split(value):
    high = value.astype(BF16)
    low = (value - high.astype(F32)).astype(BF16)
    return (high, low)


def build_one_hot(index_ref, rows, hot_ref, row_ref):
    def body(i, carry):
        index = index_ref[pl.ds(pl.multiple_of(i * GROUP, GROUP), GROUP), :]
        column = jnp.bitwise_and(index, 127) + jnp.left_shift(jnp.right_shift(index, 12), 7)
        high = jnp.where(index < 0, 99, jnp.bitwise_and(jnp.right_shift(index, 7), 31))
        column = column.astype(F32).astype(BF16)
        high = high.astype(F32).astype(BF16)
        columns = lax.broadcasted_iota(jnp.int32, (COLUMNS, LANES), 0).astype(F32).astype(BF16)
        highs = lax.broadcasted_iota(jnp.int32, (HIGH_ROWS, LANES), 0).astype(F32).astype(BF16)
        one, zero = (jnp.ones((), BF16), jnp.zeros((), BF16))
        for u in range(GROUP):
            at = pl.ds(pl.multiple_of(i * WIDE + u * LANES, LANES), LANES)
            here = jnp.broadcast_to(column[u : u + 1], (COLUMNS, LANES)) == columns
            hot_ref[:, at] = jnp.where(here, one, zero)
            here = jnp.broadcast_to(high[u : u + 1], (HIGH_ROWS, LANES)) == highs
            row_ref[:, at] = jnp.where(here, one, zero)
        return carry

    lax.fori_loop(0, rows // GROUP, body, 0, unroll=2 if rows % 16 == 0 else 1)


def make_table(source, fields, table_ref):
    for c in range(fields):
        for k, value in enumerate(split(source(c))):
            at = pl.ds((k * fields + c) * HIGH_ROWS, HIGH_ROWS)
            for b in range(2):
                part = slice(b * HIGH_ROWS, (b + 1) * HIGH_ROWS)
                table_ref[at, b * LANES : (b + 1) * LANES] = value[part]


def sum_rows(parts):
    row = lax.broadcasted_iota(jnp.int32, (GROUP, LANES), 0)

    def merge(first, second, bit):
        own = jnp.bitwise_and(row, bit) == 0
        return jnp.where(own, first, second) + pltpu.roll(jnp.where(own, second, first), bit, 0)

    parts = [merge(parts[u], parts[u + 1], 1) for u in range(0, 8, 2)]
    parts = [merge(parts[0], parts[1], 2), merge(parts[2], parts[3], 2)]
    return merge(parts[0], parts[1], 4)


def gather(table_ref, fields, rows, chunk, hot_ref, row_ref, put):
    height = fields * HIGH_ROWS

    def body(j, carry):
        start = pl.multiple_of(j * chunk * LANES, LANES)
        found = jnp.dot(
            table_ref[: 2 * height, :],
            hot_ref[:, pl.ds(start, chunk * LANES)],
            preferred_element_type=F32,
        )
        for g in range(chunk // GROUP):
            sums = [[] for c in range(fields)]
            for u in range(GROUP):
                at = (g * GROUP + u) * LANES
                lanes = slice(at, at + LANES)
                mask = row_ref[:, pl.ds(pl.multiple_of(start + at, LANES), LANES)].astype(F32)
                for c in range(fields):
                    top = c * HIGH_ROWS
                    part = found[top : top + HIGH_ROWS, lanes]
                    part = part + found[height + top : height + top + HIGH_ROWS, lanes]
                    part = part * mask
                    sums[c].append((part[0:8] + part[8:16]) + (part[16:24] + part[24:32]))
            for c in range(fields):
                put(j * (chunk // GROUP) + g, c, sum_rows(sums[c]))
        return carry

    if rows == chunk:
        body(0, 0)
    else:
        lax.fori_loop(0, rows // chunk, body, 0)


def scatter(load, rows, chunk, hot_ref, row_ref, masked_ref, total_ref):
    def body(j, carry):
        start = pl.multiple_of(j * chunk * LANES, LANES)

        def fill(i, carry):
            group = load(j * (chunk // GROUP) + i)
            for u in range(GROUP):
                at = pl.multiple_of(i * WIDE + u * LANES, LANES)
                mask = row_ref[:, pl.ds(pl.multiple_of(start + at, LANES), LANES)]
                for c in range(FIELDS):
                    for k, value in enumerate(group(u, c)):
                        top = k * TABLE + c * HIGH_ROWS
                        masked_ref[top : top + HIGH_ROWS, pl.ds(at, LANES)] = (
                            mask * jnp.broadcast_to(value, (HIGH_ROWS, LANES))
                        )
            return carry

        lax.fori_loop(0, chunk // GROUP, fill, 0, unroll=True)
        found = lax.dot_general(
            masked_ref[:, : chunk * LANES],
            hot_ref[:, pl.ds(start, chunk * LANES)],
            (((1,), (1,)), ((), ())),
            preferred_element_type=F32,
        )
        total_ref[...] += found[:TABLE] + found[TABLE:]
        return carry

    if rows == chunk:
        body(0, 0)
    else:
        lax.fori_loop(0, rows // chunk, body, 0)


def strains(grad_ref, scales, i, tile, f):
    grads = [
        [
            grad_ref[
                pl.ds(pl.multiple_of(d * POINT_ROWS + i * tile, tile), tile),
                (f * 3 + c) * LANES : (f * 3 + c + 1) * LANES,
            ]
            * scales[d]
            for d in range(3)
        ]
        for c in range(3)
    ]
    strain = {}
    for c in range(3):
        for d in range(c, 3):
            strain[c, d] = 0.5 * (grads[c][d] + grads[d][c]) if c != d else grads[c][c]
    return (strain[0, 0] + strain[1, 1] + strain[2, 2], strain)


def element_force(
    points_ref, bulk_ref, shear_ref, weight_ref, scales, keep, forward_op, backward_op,
    rhs_ref, grad_ref, flux_ref, force_ref,
):
    for c in range(FIELDS):
        high, low = split(points_ref[c])
        lanes = slice(c * LANES, (c + 1) * LANES)
        rhs_ref[0:128, lanes] = high
        rhs_ref[128:256, lanes] = low
        rhs_ref[256:384, lanes] = high
    grad_ref[...] = jnp.dot(forward_op[...], rhs_ref[...], preferred_element_type=F32)
    inverse = -keep / (scales[0] * scales[1] * scales[2])

    def body(i, carry):
        tile = 16
        at = pl.ds(pl.multiple_of(i * tile, tile), tile)
        weight = weight_ref[at, :] * inverse
        double = 2.0 * shear_ref[at, :] * weight
        lame = (bulk_ref[at, :] - 2.0 / 3.0 * shear_ref[at, :]) * weight
        for f in range(2):
            div, strain = strains(grad_ref, scales, i, tile, f)
            for c in range(3):
                for d in range(c, 3):
                    stress = double * strain[c, d]
                    if c == d:
                        stress = stress + lame * div
                    for e, g in ((c, d), (d, c))[: 1 + (c != d)]:
                        high, low = split(stress * scales[g])
                        lanes = slice((f * 3 + e) * LANES, (f * 3 + e + 1) * LANES)
                        for part, value in ((0, high), (1, low), (2, high)):
                            top = pl.multiple_of(part * 384 + g * POINT_ROWS + i * tile, tile)
                            flux_ref[pl.ds(top, tile), lanes] = value
        return carry

    lax.fori_loop(0, POINT_ROWS // 16, body, 0, unroll=8)
    force_ref[...] = jnp.dot(backward_op[...], flux_ref[...], preferred_element_type=F32)


def add_moduli_kernels(grad_ref, scales, keep, kappa_ref, mu_ref):
    def body(i, carry):
        tile = 16
        at = pl.ds(pl.multiple_of(i * tile, tile), tile)
        divs, devs = ([], [])
        for f in range(2):
            div, strain = strains(grad_ref, scales, i, tile, f)
            third = div / 3.0
            divs.append(div)
            devs.append({k: v - third if k[0] == k[1] else v for k, v in strain.items()})
        even = sum(devs[0][c, c] * devs[1][c, c] for c in range(3))
        odd = sum(devs[0][key] * devs[1][key] for key in ((0, 1), (0, 2), (1, 2)))
        kappa_ref[at, :] += time_step * divs[0] * divs[1] * keep
        mu_ref[at, :] += 2.0 * time_step * (even + 2.0 * odd) * keep
        return carry

    lax.fori_loop(0, POINT_ROWS // 16, body, 0, unroll=8)


def partners():
    row, col = (lax.axis_index("row"), lax.axis_index("col"))
    rows, cols = (lax.axis_size("row"), lax.axis_size("col"))

    def at(offset):
        return (
            lax.rem(row + offset[0] + rows, rows),
            lax.rem(col + offset[1] + cols, cols),
        )

    messages = []
    for s in range(4):
        messages.append((pl.ds(s * 6, 5), pl.ds(face_opposite[s] * 6, 5), at(face_offsets[s])))
    for s in range(4):
        messages.append(
            (pl.ds(s * 6 + 5, 1), pl.ds(edge_opposite[s] * 6 + 5, 1), at(edge_offsets[s]))
        )
    return messages


def kernel(
    steps, count_hbm, face_len_hbm, edge_len_hbm,
    fwd_hbm, fwd_prev_hbm, adj_hbm, adj_prev_hbm, mass_hbm, ibool_hbm, jac_hbm, kap_hbm, mod_hbm,
    face_hbm, edge_hbm, rec_hbm, src_hbm, forward_hbm, backward_hbm, weight_hbm,
    packed,
    count_ref, face_len_ref, edge_len_ref,
    fwd_ref, fwd_prev_ref, adj_ref, adj_prev_ref, mass_ref, ibool_ref, jac_ref, kap_ref, mod_ref,
    face_ref, edge_ref, rec_ref, src_ref, forward_op, backward_op, weight_ref,
    now, prev, density, index, list_index, hot, row_hot, list_hot, list_row, table, points,
    bulk, shear, rhs, grad, flux, force, masked, total, kappa_sum, mu_sum, send, recv,
    in_sem, send_sem, recv_sem,
):
    arrivals = []
    for source, target in (
        (ibool_hbm, ibool_ref), (count_hbm, count_ref), (face_len_hbm, face_len_ref),
        (edge_len_hbm, edge_len_ref), (face_hbm, face_ref), (edge_hbm, edge_ref), (fwd_hbm, fwd_ref),
        (adj_hbm, adj_ref), (fwd_prev_hbm, fwd_prev_ref), (adj_prev_hbm, adj_prev_ref),
        (kap_hbm, kap_ref), (mod_hbm, mod_ref), (jac_hbm, jac_ref), (weight_hbm, weight_ref),
        (forward_hbm, forward_op), (backward_hbm, backward_op), (rec_hbm, rec_ref),
        (src_hbm, src_ref), (mass_hbm, mass_ref),
    ):
        copy = pltpu.make_async_copy(source, target, in_sem.at[len(arrivals)])
        copy.start()
        arrivals.append(copy)

    messages = partners()
    barrier = pltpu.get_barrier_semaphore()
    for _, _, device in messages:
        pl.semaphore_signal(barrier, inc=1, device_id=device, device_id_type=MESH)

    lane = lax.broadcasted_iota(jnp.int32, (1, LANES), 1)
    index[...] = jnp.full((POINT_ROWS, LANES), -1, jnp.int32)
    list_index[...] = jnp.full((LIST_ROWS, LANES), -1, jnp.int32)
    bulk[...] = jnp.zeros((POINT_ROWS, LANES), F32)
    shear[...] = jnp.zeros((POINT_ROWS, LANES), F32)
    density[...] = jnp.zeros((64, LANES), F32)
    kappa_sum[...] = jnp.zeros((POINT_ROWS, LANES), F32)
    mu_sum[...] = jnp.zeros((POINT_ROWS, LANES), F32)
    send[...] = jnp.zeros(send.shape, F32)

    arrivals[0].wait()
    index[0:125, :] = ibool_ref[...]
    build_one_hot(index, POINT_ROWS, hot, row_hot)
    for copy in arrivals[1:]:
        copy.wait()

    count = jnp.broadcast_to(count_ref[...], (1, LANES))
    keep = jnp.where(lane < count, 1.0, 0.0).astype(F32)
    width = edge_ref.shape[2]
    narrow = lax.broadcasted_iota(jnp.int32, (1, width), 1)
    for s in range(4):
        for k in range(5):
            nodes = face_ref[0, s : s + 1, k * LANES : (k + 1) * LANES]
            live = lane + k * LANES < jnp.broadcast_to(face_len_ref[:, s : s + 1], (1, LANES))
            list_index[s * 6 + k : s * 6 + k + 1, :] = jnp.where(live, nodes, -1)
        nodes = edge_ref[0, s : s + 1, :]
        live = narrow < jnp.broadcast_to(edge_len_ref[:, s : s + 1], (1, width))
        list_index[s * 6 + 5 : s * 6 + 6, 0:width] = jnp.where(live, nodes, -1)
    build_one_hot(list_index, LIST_ROWS, list_hot, list_row)
    bulk[0:125, :] = kap_ref[...]
    shear[0:125, :] = mod_ref[...]

    def spread(r, carry):
        at = pl.ds(pl.multiple_of(r * LANES, LANES), LANES)
        for base, target, source in (
            (0, now, fwd_ref), (3, now, adj_ref), (0, prev, fwd_prev_ref), (3, prev, adj_prev_ref),
        ):
            value = source[:, at]
            for c in range(3):
                target[base + c, pl.ds(r, 1), :] = value[c : c + 1]
        return carry

    lax.fori_loop(0, 64, spread, 0, unroll=8)

    element = lax.broadcasted_iota(jnp.int32, (LANES, LANES), 0)
    chosen = jnp.where(
        jnp.broadcast_to(rec_ref[...], (LANES, LANES)) == element, 1.0, 0.0
    ).astype(BF16)

    def put_point(i, c, value):
        points[c, pl.ds(pl.multiple_of(i * GROUP, GROUP), GROUP), :] = value

    scales = [jac_ref[d : d + 1, :] for d in range(3)]
    pl.semaphore_wait(barrier, len(messages))

    def one_step(step, carry):
        make_table(lambda c: now[c], FIELDS, table)
        gather(table, FIELDS, POINT_ROWS, GATHER_ROWS, hot, row_hot, put_point)
        element_force(
            points, bulk, shear, weight_ref, scales, keep, forward_op, backward_op,
            rhs, grad, flux, force,
        )
        for c in range(3):
            source = src_ref[c, pl.ds(step, 1), :]
            high, low = split(source)
            rest = source - high.astype(F32) - low.astype(F32)
            stack = jnp.concatenate(
                [
                    jnp.broadcast_to(part.astype(F32), (8, LANES))
                    for part in (high, low, rest)
                ],
                0,
            ).astype(BF16)
            found = lax.dot_general(
                stack, chosen, (((1,), (1,)), ((), ())), preferred_element_type=F32
            )
            lanes = slice((3 + c) * LANES, (4 + c) * LANES)
            force[62:63, lanes] += found[0:1] + found[8:9] + found[16:17]

        def load_point(i):
            at = pl.ds(pl.multiple_of(i * GROUP, GROUP), GROUP)
            blocks = [split(force[at, c * LANES : (c + 1) * LANES]) for c in range(FIELDS)]
            return lambda u, c: [part[u : u + 1] for part in blocks[c]]

        total[...] = jnp.zeros((TABLE, COLUMNS), F32)
        scatter(load_point, POINT_ROWS, SCATTER_ROWS, hot, row_hot, masked, total)
        high, low = split(total[...])
        table[:TABLE, :] = high
        table[TABLE:, :] = low

        def put_list(i, c, value):
            for u in range(GROUP):
                send[step, i * GROUP + u, c : c + 1, :] = value[u : u + 1]

        gather(table, FIELDS, LIST_ROWS, LIST_ROWS, list_hot, list_row, put_list)

        copies = []
        for slot, (source, target, device) in enumerate(messages):
            landing = face_opposite[slot] if slot < 4 else 4 + edge_opposite[slot - 4]
            copy = pltpu.make_async_remote_copy(
                src_ref=send.at[step, source],
                dst_ref=recv.at[step, target],
                send_sem=send_sem.at[step, slot],
                recv_sem=recv_sem.at[step, landing],
                device_id=device,
                device_id_type=MESH,
            )
            copy.start()
            copies.append(copy)
        add_moduli_kernels(grad, scales, keep, kappa_sum, mu_sum)
        for copy in copies:
            copy.wait_recv()

        def load_list(i):
            blocks = [split(recv[step, i * GROUP + u]) for u in range(GROUP)]
            return lambda u, c: [part[c : c + 1] for part in blocks[u]]

        scatter(load_list, LIST_ROWS, LIST_ROWS, list_hot, list_row, masked, total)

        for b in range(2):
            part = pl.ds(b * HIGH_ROWS, HIGH_ROWS)
            lanes = slice(b * LANES, (b + 1) * LANES)
            mass = mass_ref[part, :]
            accel = [
                mass * total[c * HIGH_ROWS : (c + 1) * HIGH_ROWS, lanes] for c in range(FIELDS)
            ]
            both = 0.0
            for c in range(3):
                both = both + accel[3 + c] * now[c, part, :]
            density[part, :] += time_step * both
            for c in range(FIELDS):
                field = now[c, part, :]
                later = 2.0 * field - prev[c, part, :] + time_step * time_step * accel[c]
                prev[c, part, :] = field
                now[c, part, :] = later
        for copy in copies:
            copy.wait_send()
        return carry

    lax.fori_loop(0, steps, one_step, 0)

    make_table(lambda c: density[...], 1, table)
    gather(table, 1, POINT_ROWS, GATHER_ROWS, hot, row_hot, put_point)
    for c in range(FIELDS):
        packed[c * 64 : (c + 1) * 64, :] = now[c]
    for k, value in enumerate((points[0] * keep, kappa_sum[...], mu_sum[...])):
        packed[FIELDS * 64 + k * POINT_ROWS : FIELDS * 64 + (k + 1) * POINT_ROWS, :] = value


def unpack(
    packed, fwd_out, adj_out, rho_out, kappa_out, mu_out, fwd, adj, rho, kappa, mu, out_sem
):
    copies = []
    for k, (source, target) in enumerate(((rho, rho_out), (kappa, kappa_out), (mu, mu_out))):
        top = FIELDS * 64 + k * POINT_ROWS
        source[...] = packed[top : top + 125, :]
        copies.append(pltpu.make_async_copy(source, target, out_sem.at[k]))
        copies[k].start()
    for k, (source, target) in enumerate(((fwd, fwd_out), (adj, adj_out))):
        for c in range(3):

            def join(i, carry):
                top = (k * 3 + c) * 64 + i * GROUP
                rows = packed[pl.ds(pl.multiple_of(top, GROUP), GROUP), :]
                for u in range(GROUP):
                    at = pl.ds(pl.multiple_of(i * WIDE + u * LANES, LANES), LANES)
                    source[c : c + 1, at] = rows[u : u + 1]
                return carry

            lax.fori_loop(0, 64 // GROUP, join, 0, unroll=True)
        copies.append(pltpu.make_async_copy(source, target, out_sem.at[3 + k]))
        copies[3 + k].start()
    for copy in copies:
        copy.wait()


def on_device(
    fwd_now, fwd_prev, adj_now, adj_prev, inv_mass, ibool, inv_jac, kappa, mu, elem_count,
    face_nodes, face_len, edge_nodes, edge_len, rec_elem, adj_src,
):
    forward_op, backward_op, weight = operators()
    steps = adj_src.shape[0]
    nodes = fwd_now.shape[1]
    elements = ibool.shape[1]
    vmem = pl.BlockSpec(memory_space=pltpu.VMEM)
    spread = POINT_ROWS * LANES
    listed = LIST_ROWS * LANES
    operands = (
        elem_count.reshape(1, 1), face_len, edge_len,
        fwd_now, fwd_prev, adj_now, adj_prev, inv_mass.reshape(64, LANES), ibool, inv_jac, kappa, mu,
        face_nodes, edge_nodes, rec_elem.reshape(1, elements), adj_src.transpose(1, 0, 2),
        forward_op, backward_op, weight,
    )
    scratch = [pltpu.VMEM(operand.shape, operand.dtype) for operand in operands] + [
        pltpu.VMEM((FIELDS, 64, LANES), F32),
        pltpu.VMEM((FIELDS, 64, LANES), F32),
        pltpu.VMEM((64, LANES), F32),
        pltpu.VMEM((POINT_ROWS, LANES), jnp.int32),
        pltpu.VMEM((LIST_ROWS, LANES), jnp.int32),
        pltpu.VMEM((COLUMNS, spread), BF16),
        pltpu.VMEM((HIGH_ROWS, spread), BF16),
        pltpu.VMEM((COLUMNS, listed), BF16),
        pltpu.VMEM((HIGH_ROWS, listed), BF16),
        pltpu.VMEM((2 * TABLE, COLUMNS), BF16),
        pltpu.VMEM((FIELDS, POINT_ROWS, LANES), F32),
        pltpu.VMEM((POINT_ROWS, LANES), F32),
        pltpu.VMEM((POINT_ROWS, LANES), F32),
        pltpu.VMEM((384, FIELDS * LANES), BF16),
        pltpu.VMEM((384, FIELDS * LANES), F32),
        pltpu.VMEM((3 * 384, FIELDS * LANES), BF16),
        pltpu.VMEM((POINT_ROWS, FIELDS * LANES), F32),
        pltpu.VMEM((2 * TABLE, SCATTER_ROWS * LANES), BF16),
        pltpu.VMEM((TABLE, COLUMNS), F32),
        pltpu.VMEM((POINT_ROWS, LANES), F32),
        pltpu.VMEM((POINT_ROWS, LANES), F32),
        pltpu.VMEM((steps, LIST_ROWS, 8, LANES), F32),
        pltpu.VMEM((steps, LIST_ROWS, 8, LANES), F32),
        pltpu.SemaphoreType.DMA((len(operands),)),
        pltpu.SemaphoreType.DMA((steps, 8)),
        pltpu.SemaphoreType.DMA((steps, 8)),
    ]
    point = jax.ShapeDtypeStruct((125, elements), F32)
    node = jax.ShapeDtypeStruct((3, nodes), F32)
    hbm = pl.BlockSpec(memory_space=pl.ANY)
    packed = pl.pallas_call(
        functools.partial(kernel, steps),
        out_shape=jax.ShapeDtypeStruct((FIELDS * 64 + 3 * POINT_ROWS, LANES), F32),
        in_specs=[hbm] * len(operands),
        out_specs=vmem,
        scratch_shapes=scratch,
        compiler_params=pltpu.CompilerParams(
            collective_id=0, has_side_effects=True, vmem_limit_bytes=60 << 20
        ),
    )(*operands)
    outs = (node, node, point, point, point)
    return pl.pallas_call(
        unpack,
        out_shape=outs,
        in_specs=[vmem],
        out_specs=(hbm,) * 5,
        scratch_shapes=[pltpu.VMEM(out.shape, F32) for out in outs]
        + [pltpu.SemaphoreType.DMA((len(outs),))],
        compiler_params=pltpu.CompilerParams(vmem_limit_bytes=60 << 20),
    )(packed)


def solution(mesh):
    field = P(None, ("row", "col"))
    part = P(("row", "col"))
    in_specs = (
        field, field, field, field, part, field, field, field, field, part,
        P(("row", "col"), None, None), P(("row", "col"), None),
        P(("row", "col"), None, None), P(("row", "col"), None),
        part, P(None, None, ("row", "col")),
    )
    return jax.shard_map(
        on_device, mesh=mesh, in_specs=in_specs, out_specs=(field,) * 5, check_vma=False
    )
```
